256 devices in a mesh: dp: 16 (over z_lo, x), tensor: 16 (over y, z_hi, core).
Axes of the slice: x: 4, y: 4, z: 8 (z_hi: 2, z_lo: 4; z = z_hi * 4 + z_lo), core: 2. Of those that a mesh axis runs over, the one named last changes fastest.
Arguments:
- hidden_rows: bfloat16 [16, 256, 14336], P('dp', 'tensor'), may hold values from -6 to 6
- out_grad: bfloat16 [16, 256, 4096], P('dp', None, 'tensor'), may hold values from -0.5 to 0.5
- down_weight: bfloat16 [14336, 4096], P('dp', 'tensor'), may hold values from -4 to 4
- query_init: float32 [64, 4096], P(None, 'tensor'), may hold values from -6 to 6
Outputs:
- input_grad: bfloat16 [16, 256, 14336], P('dp', 'tensor')
- q_factor: float32 [64, 4096], P(None, 'tensor')
- error_new: bfloat16 [16, 14336, 4096], P('dp', None, 'tensor')
The draws below stay inside these ranges and needn't reach their ends.
All inputs are finite; a program needn't handle non-finite values.
Results may differ from the reference program's by a relative error of at most 0.017.
Values may be sent and summed in bfloat16 or wider, within the bound.
No kernel may reach another device: no remote copies, remote signals or barrier semaphores. Data moves between devices by JAX's collectives and lax.ppermute only.
A program may use at most 128 MiB of HBM per device.

```python
import jax
import jax.numpy as jnp
from jax import lax

D = 4096
FF = 14336
RANK = 64
GTOK = 256
N_DP = 16
N_TENSOR = 16


def with_spikes(drawn, stream_key, source, target, shards_of, factor):
    owner, partner = [(jnp.arange(drawn.shape[position]) // (drawn.shape[position] // shards_of)).reshape([-1 if axis == position else 1 for axis in range(drawn.ndim)]) for position in (source, target)]
    chosen = jax.random.permutation(stream_key, shards_of)[partner]
    strong = (owner == chosen) | (owner == (partner + shards_of // 2) % shards_of)
    return jnp.where(strong, factor * drawn, drawn)


def level_of(stream_key, extent, pieces, least, top_value):
    gain, own = 1.0, jax.random.fold_in(stream_key, 6)
    for position, blocks in pieces:
        heights = jnp.exp(jax.random.uniform(jax.random.fold_in(own, position), (blocks,), jnp.float32, least / len(pieces), top_value / len(pieces)))
        gain = gain * jnp.repeat(heights, extent[position] // blocks).reshape([-1 if axis == position else 1 for axis in range(len(extent))])
    return gain


def bell_draw(key, shape, width, limit, pieces=(), kind=jnp.bfloat16):
    result = width * jax.random.normal(key, shape, jnp.float32)
    if pieces:
        result = result * level_of(key, shape, pieces, -0.22, 0.18)
    return jnp.clip(result, -limit, limit).astype(kind)


def gaussian_with(key, extent, scale, limit, pieces, heavy, kind=jnp.bfloat16):
    result = scale * jax.random.normal(key, extent, jnp.float32)
    if pieces:
        result = result * level_of(key, extent, pieces, -0.22, 0.18)
    return jnp.clip(with_spikes(result, jax.random.fold_in(key, 3), *heavy), -limit, limit).astype(kind)


def setup_inputs(seed: int = 0) -> dict:
    streams_of = jax.random.split(jax.random.key(seed), 5)
    hidden_rows = bell_draw(streams_of[0], (N_DP, GTOK, FF), 1.0, 6.0, ((0, 16), (1, 16)))
    out_grad = gaussian_with(streams_of[1], (N_DP, GTOK, D), GTOK ** -0.5, 0.5, ((0, 16), (2, 16)), (2, 1, 16, 2.0))
    down_weight = bell_draw(streams_of[2], (FF, D), (GTOK ** 0.5 * D ** -0.5), 4.0, ((0, 16), (1, 16)))
    query_init = bell_draw(streams_of[3], (RANK, D), 1.0, 6.0, ((1, 16),), jnp.float32)
    return {"hidden_rows": hidden_rows, "out_grad": out_grad, "down_weight": down_weight, "query_init": query_init}


def reference(hidden_rows, out_grad, down_weight, query_init):
    local_cols = D // N_TENSOR
    grad_shards = jnp.moveaxis(out_grad.reshape(N_DP, GTOK, N_TENSOR, local_cols), 2, 0)
    weight_shards = jnp.moveaxis(down_weight.reshape(FF, N_TENSOR, local_cols), 1, 0)

    def add_shard(total, pair):
        grad_part, weight_part = pair
        term = jnp.einsum('gtd,fd->gtf', grad_part.astype(jnp.float32), weight_part.astype(jnp.float32))
        term = lax.optimization_barrier(term.astype(jnp.bfloat16))
        return (total + term.astype(jnp.float32), None)
    summed, _ = lax.scan(add_shard, jnp.zeros((N_DP, GTOK, FF), jnp.float32), (grad_shards, weight_shards))
    input_grad = summed.astype(jnp.bfloat16)
    weight_grad = jnp.einsum('gtf,gtd->gfd', hidden_rows.astype(jnp.float32), out_grad.astype(jnp.float32))
    merged = weight_grad.reshape(N_DP, FF, N_TENSOR, local_cols)
    query_blocks = query_init.reshape(RANK, N_TENSOR, local_cols)
    highest = lax.Precision.HIGHEST
    left = jnp.einsum('gfkd,rkd->krf', merged, query_blocks, precision=highest) / N_DP
    gram = jnp.einsum('krf,ksf->krs', left, left, precision=highest)
    lower = jnp.linalg.cholesky(gram)
    ortho = lax.linalg.triangular_solve(lower, left, left_side=True, lower=True)
    right = jnp.einsum('gfkd,krf->rkd', merged, ortho, precision=highest) / N_DP
    approx = jnp.einsum('krf,rkd->fkd', ortho, right, precision=highest)
    error_new = (merged - approx[None]).reshape(N_DP, FF, D).astype(jnp.bfloat16)
    return (input_grad, right.reshape(RANK, D), error_new)
```

```python
import functools

import jax
import jax.numpy as jnp
from jax import lax
from jax.experimental import pallas as pl
from jax.experimental.pallas import tpu as pltpu
from jax.sharding import Mesh
from jax.sharding import PartitionSpec as P

AXES = ("zl", "x", "y", "zh", "c")
SIZES = (4, 4, 4, 2, 2)
F = 14336
BLOCK = 896
RANK = 64
TOKENS = 256
COLS = 256
STEP = 2048
PART = 128
BF = jnp.bfloat16
F32 = jnp.float32
HIGH = lax.Precision.HIGHEST
SWAP = ((0, 1), (1, 0))
VMEM = pl.BlockSpec(memory_space=pltpu.VMEM)
SMEM = pl.BlockSpec(memory_space=pltpu.SMEM)
LIMIT = pltpu.CompilerParams(vmem_limit_bytes=24 * 2**20)


def shift(s):
    return tuple((i, (i + s) % 4) for i in range(4))


def flip(s):
    return tuple((i, i ^ s) for i in range(4))


def ring3(value, axis):
    return [lax.ppermute(value, axis, shift(-s)) for s in (1, 2, 3)]


def flip3(value):
    return [lax.ppermute(value, "zl", flip(s)) for s in (1, 2, 3)]


def after(value, *others):
    return lax.optimization_barrier((value, *others))[0]


def dot(a, b, ca, cb):
    return lax.dot_general(a, b, (((ca,), (cb,)), ((), ())), preferred_element_type=F32)


def thirds(value):
    parts = []
    for _ in range(3):
        parts.append(value.astype(BF))
        value = value - parts[-1].astype(F32)
    return parts


def call(kernel, shapes, tables, arrays, flops, name):
    nbytes = sum(a.size * a.dtype.itemsize for a in arrays)
    return pl.pallas_call(
        kernel,
        out_shape=[jax.ShapeDtypeStruct(s, d) for s, d in shapes],
        in_specs=[SMEM] * len(tables) + [VMEM] * len(arrays),
        out_specs=[VMEM] * len(shapes),
        compiler_params=LIMIT,
        cost_estimate=pl.CostEstimate(flops=flops, bytes_accessed=nbytes, transcendentals=0),
        name=name,
    )(*tables, *arrays)


def prepare_kernel(order, grad, query, rows_ref, a_ref):
    for i in range(16):
        rows_ref[16 * i : 16 * i + 16, :] = grad[order[i]]
    rows = rows_ref[...]
    a = sum(dot(q, rows, 1, 1) for q in reversed(thirds(query[...])))
    high = a.astype(BF)
    a_ref[:RANK, :] = high
    a_ref[RANK:, :] = (a - high.astype(F32)).astype(BF)


def lay_kernel(blocks, out_ref):
    for j in range(16):
        out_ref[:, BLOCK * j : BLOCK * (j + 1)] = blocks[j]


def left_kernel(table, a_ref, *refs):
    hidden, outs = refs[:4], refs[4:]
    a = a_ref[...]
    for r in range(4):
        for p in range(4):
            here = pl.ds(pl.multiple_of(table[4 * r + p] * BLOCK, 128), BLOCK)
            both = dot(a, jnp.concatenate([h[:, here] for h in hidden], axis=0), 1, 0)
            outs[r][p] = (both[:RANK] + both[RANK:]).astype(BF)


def sum_kernel(a, b, c, d, own, *outs):
    for p in range(4):
        total = (a[p].astype(F32) + b[p].astype(F32)) + (c[p].astype(F32) + d[p].astype(F32))
        if p == 0:
            own[...] = total
        else:
            outs[p - 1][...] = total.astype(BF)


def stats_kernel(table, *refs):
    lefts, hidden, grad = refs[:4], refs[4:8], refs[8]
    left_ref, local_ref, gram_ref = refs[9:]
    total = jnp.zeros((TOKENS + RANK, RANK), F32)
    for r in range(4):
        for p in range(4):
            here = pl.ds(pl.multiple_of(table[4 * r + p] * BLOCK, 128), BLOCK)
            block = lefts[r][p]
            total += dot(jnp.concatenate([h[:, here] for h in hidden] + [block], axis=0), block, 1, 1)
            left_ref[:, here] = block
    gram_ref[...] = total[TOKENS:]
    local_ref[...] = sum(dot(t, grad[...], 0, 0) for t in reversed(thirds(total[:TOKENS])))


def inverse_kernel(gram, out_ref):
    row_of = lax.broadcasted_iota(jnp.int32, (RANK, 1), 0)
    eye = lax.broadcasted_iota(jnp.int32, (RANK, RANK), 0) == lax.broadcasted_iota(jnp.int32, (RANK, RANK), 1)
    both = jnp.concatenate([gram[...], eye.astype(F32)], axis=1)
    for k in range(RANK):
        pivot = both[k : k + 1, k : k + 1]
        factor = jnp.where(row_of > k, both[:, k : k + 1] / pivot, 0.0)
        scale = jnp.where(row_of == k, lax.rsqrt(pivot), 1.0)
        both = both * scale - factor * both[k : k + 1, :]
    out_ref[...] = both[:, RANK:]


def error_kernel(inverse, s0, s1, s2, s3, grad, left, h0, h1, h2, h3, right_ref, out_ref, weights):
    @pl.when(pl.program_id(0) == 0)
    def _():
        summed = (s0[...] + s1[...]) + (s2[...] + s3[...])
        inv = inverse[...]
        right = lax.dot_general(
            inv, summed, (((1,), (0,)), ((), ())), precision=HIGH, preferred_element_type=F32
        ) * (1.0 / 16)
        right_ref[...] = right
        m = -lax.dot_general(inv, right, (((0,), (0,)), ((), ())), precision=HIGH, preferred_element_type=F32)
        high = m.astype(BF)
        weights[:TOKENS, :] = grad[...]
        weights[TOKENS : TOKENS + RANK, :] = high
        weights[TOKENS + RANK :, :] = (m - high.astype(F32)).astype(BF)

    block = left[...]
    rows = jnp.concatenate([h0[...], h1[...], h2[...], h3[...], block, block], axis=0)
    out_ref[...] = dot(rows, weights[...], 0, 0).astype(BF)


def error_of(inverse, sums, grad, left, hidden):
    def whole(a):
        return pl.BlockSpec(a.shape, lambda i: (0, 0))

    def some(a):
        return pl.BlockSpec((a.shape[0], STEP), lambda i: (0, i))

    return pl.pallas_call(
        error_kernel,
        out_shape=(jax.ShapeDtypeStruct((RANK, COLS), F32), jax.ShapeDtypeStruct((F, COLS), BF)),
        grid=(F // STEP,),
        in_specs=[whole(inverse)] + [whole(s) for s in sums] + [whole(grad), some(left)] + [some(h) for h in hidden],
        out_specs=(
            pl.BlockSpec((RANK, COLS), lambda i: (0, 0)),
            pl.BlockSpec((STEP, COLS), lambda i: (i, 0)),
        ),
        scratch_shapes=[pltpu.VMEM((TOKENS + 2 * RANK, COLS), BF)],
        compiler_params=LIMIT,
        cost_estimate=pl.CostEstimate(
            flops=2 * (TOKENS + 2 * RANK) * F * COLS,
            bytes_accessed=2 * (TOKENS + RANK + COLS) * F,
            transcendentals=0,
        ),
        name="error_new",
    )(inverse, *sums, grad, left, *hidden)


def input_kernel(group, t0, t1, t2, t3, weight, out_ref):
    total = jnp.zeros((TOKENS, PART), F32)
    for d in range(16):
        rows = jnp.concatenate([t[:, d].reshape(64, COLS) for t in (t0, t1, t2, t3)], axis=0)
        total += dot(rows, weight[d], 1, 1)
    total = total.astype(BF).reshape(16, 16, PART)
    for i in range(16):
        out_ref[group[i]] = total[i]


def input_of(group, tokens, weight):
    return pl.pallas_call(
        input_kernel,
        out_shape=jax.ShapeDtypeStruct((16, 16, BLOCK), BF),
        grid=(BLOCK // PART,),
        in_specs=[SMEM]
        + [pl.BlockSpec(t.shape, lambda i: (0, 0, 0, 0)) for t in tokens]
        + [pl.BlockSpec((16, PART, COLS), lambda i: (0, i, 0))],
        out_specs=pl.BlockSpec((16, 16, PART), lambda i: (0, 0, i)),
        compiler_params=LIMIT,
        cost_estimate=pl.CostEstimate(
            flops=2 * TOKENS * 16 * COLS * BLOCK, bytes_accessed=10 * 2**20, transcendentals=0
        ),
        name="input_grad",
    )(group, *tokens, weight)


def on_device(hidden_rows, out_grad, down_weight, query_init):
    zl, x, y, zh, c = (lax.axis_index(a) for a in AXES)
    four = jnp.arange(4)
    ahead = (y + four) % 4
    grad = out_grad[0]
    mine = hidden_rows[0]

    with jax.named_scope("prepare"):
        order = jnp.concatenate([ahead * 4 + h * 2 + k for k in (c, 1 - c) for h in (zh, 1 - zh)]).astype(jnp.int32)
        grad_rows, a = call(
            prepare_kernel,
            [((TOKENS, COLS), BF), ((2 * RANK, TOKENS), BF)],
            [order],
            [grad.reshape(16, 16, COLS), query_init],
            2 * 3 * RANK * TOKENS * COLS,
            "prepare",
        )

    with jax.named_scope("hidden_gather"):
        other = lax.ppermute(mine, "zh", SWAP)
        rest = ring3(mine, "y")
        near = jnp.concatenate([mine] + rest, axis=0)
        far = jnp.concatenate([other] + ring3(after(other, near, a), "y"), axis=0)
        hidden = [near, far, lax.ppermute(near, "c", SWAP)]

    with jax.named_scope("weight_gather"):
        weight = lax.all_gather(down_weight, ("y", "zh", "c"))

    with jax.named_scope("grad_gather"):
        tokens = lax.all_to_all(grad.reshape(16, 16, COLS), ("y", "zh", "c"), 0, 0)
        tokens = jnp.stack([tokens] + flip3(tokens))
        far, tokens = lax.optimization_barrier((far, tokens))
        hidden = [near, far, hidden[2], lax.ppermute(far, "c", SWAP)]

    table = (((x + four) % 4)[:, None] * 4 + (zl ^ four)[None, :]).reshape(16).astype(jnp.int32)
    with jax.named_scope("left_reduce"):
        parts = call(
            left_kernel,
            [((4, RANK, BLOCK), BF)] * 4,
            [table],
            [a, *hidden],
            2 * 2 * RANK * TOKENS * F,
            "left",
        )
        parts = [parts[0]] + [lax.ppermute(parts[r], "x", shift(r)) for r in (1, 2, 3)]
        block, *sends = call(
            sum_kernel,
            [((RANK, BLOCK), F32)] + [((RANK, BLOCK), BF)] * 3,
            [],
            parts,
            16 * RANK * BLOCK,
            "sum",
        )
        ready = after(tokens, sends[0])
        token1, token3 = (lax.ppermute(ready, "x", shift(-s)) for s in (1, 3))
        for s in (1, 2, 3):
            block = block + lax.ppermute(sends[s - 1], "zl", flip(s)).astype(F32)
        block, token1, token3 = lax.optimization_barrier(((block * (1.0 / 16)).astype(BF), token1, token3))
    with jax.named_scope("left_gather"):
        token2 = lax.ppermute(after(tokens, block), "x", shift(-2))
        column = jnp.stack([block] + flip3(block))
        column, token2 = lax.optimization_barrier((column, token2))
        lefts = [column] + ring3(column, "x")

    with jax.named_scope("input_grad"):
        group = ((zl ^ four)[None, :] * 4 + ((x + four) % 4)[:, None]).reshape(16).astype(jnp.int32)
        partial = input_of(group, [after(tokens, column), token1, token2, token3], weight)
        lefts, _ = lax.optimization_barrier((lefts, partial))

    with jax.named_scope("stats"):
        left, local, gram = call(
            stats_kernel,
            [((RANK, F), BF), ((RANK, COLS), F32), ((RANK, RANK), F32)],
            [table],
            [*lefts, *hidden, grad_rows],
            2 * RANK * (TOKENS + RANK) * F,
            "stats",
        )
    with jax.named_scope("right"):
        for v in ring3(local, "x"):
            local = local + v
        sums = [local] + flip3(local)
        inverse = call(inverse_kernel, [((RANK, RANK), F32)], [], [after(gram, local)], 64 * 64 * 128 * 2, "inverse")[0]
    with jax.named_scope("error_new"):
        right, error_new = error_of(inverse, sums, grad_rows, left, hidden)

    with jax.named_scope("input_grad"):
        summed = lax.all_to_all(partial, ("zl", "x"), 0, 0)
        input_grad = call(lay_kernel, [((16, F), BF)], [], [summed], 16 * F, "lay")[0][None]
    return input_grad, right, error_new[None]


def solution(mesh):
    fine = Mesh(mesh.devices.reshape(SIZES), AXES)
    dp, tensor = ("zl", "x"), ("y", "zh", "c")
    return jax.shard_map(
        on_device,
        mesh=fine,
        in_specs=(P(dp, tensor, None), P(dp, None, tensor), P(dp, tensor), P(None, tensor)),
        out_specs=(P(dp, tensor, None), P(None, tensor), P(dp, None, tensor)),
        check_vma=False,
    )
```

```python
import functools

import jax
import jax.numpy as jnp
from jax import lax
from jax.experimental import pallas as pl
from jax.experimental.pallas import tpu as pltpu
from jax.sharding import Mesh
from jax.sharding import PartitionSpec as P

AXES = ("zl", "x", "y", "zh", "c")
SIZES = (4, 4, 4, 2, 2)
F = 14336
BLOCK = 896
RANK = 64
TOKENS = 256
COLS = 256
STEP = 3584
PART = 128
BF = jnp.bfloat16
F32 = jnp.float32
HIGH = lax.Precision.HIGHEST
SWAP = ((0, 1), (1, 0))
VMEM = pl.BlockSpec(memory_space=pltpu.VMEM)
SMEM = pl.BlockSpec(memory_space=pltpu.SMEM)
LIMIT = pltpu.CompilerParams(vmem_limit_bytes=24 * 2**20)


def shift(s):
    return tuple((i, (i + s) % 4) for i in range(4))


def flip(s):
    return tuple((i, i ^ s) for i in range(4))


def ring3(value, axis):
    return [lax.ppermute(value, axis, shift(-s)) for s in (1, 2, 3)]


def flip3(value):
    return [lax.ppermute(value, "zl", flip(s)) for s in (1, 2, 3)]


def after(value, *others):
    return lax.optimization_barrier((value, *others))[0]


def dot(a, b, ca, cb):
    return lax.dot_general(a, b, (((ca,), (cb,)), ((), ())), preferred_element_type=F32)


def thirds(value):
    parts = []
    for _ in range(3):
        parts.append(value.astype(BF))
        value = value - parts[-1].astype(F32)
    return parts


def call(kernel, shapes, tables, arrays, flops, name):
    nbytes = sum(a.size * a.dtype.itemsize for a in arrays)
    return pl.pallas_call(
        kernel,
        out_shape=[jax.ShapeDtypeStruct(s, d) for s, d in shapes],
        in_specs=[SMEM] * len(tables) + [VMEM] * len(arrays),
        out_specs=[VMEM] * len(shapes),
        compiler_params=LIMIT,
        cost_estimate=pl.CostEstimate(flops=flops, bytes_accessed=nbytes, transcendentals=0),
        name=name,
    )(*tables, *arrays)


def prepare_kernel(order, grad, query, rows_ref, a_ref):
    for i in range(16):
        rows_ref[16 * i : 16 * i + 16, :] = grad[order[i]]
    rows = rows_ref[...]
    a = sum(dot(q, rows, 1, 1) for q in reversed(thirds(query[...])))
    high = a.astype(BF)
    a_ref[:RANK, :] = high
    a_ref[RANK:, :] = (a - high.astype(F32)).astype(BF)


def lay_kernel(blocks, out_ref):
    for j in range(16):
        out_ref[:, BLOCK * j : BLOCK * (j + 1)] = blocks[j]


def left_kernel(table, a_ref, *refs):
    hidden, outs = refs[:4], refs[4:]
    a = a_ref[...]
    for r in range(4):
        for p in range(4):
            here = pl.ds(pl.multiple_of(table[4 * r + p] * BLOCK, 128), BLOCK)
            both = dot(a, jnp.concatenate([h[:, here] for h in hidden], axis=0), 1, 0)
            outs[r][p] = (both[:RANK] + both[RANK:]).astype(BF)


def sum_kernel(a, b, c, d, own, *outs):
    for p in range(4):
        total = (a[p].astype(F32) + b[p].astype(F32)) + (c[p].astype(F32) + d[p].astype(F32))
        if p == 0:
            own[...] = total
        else:
            outs[p - 1][...] = total.astype(BF)


def stats_kernel(table, *refs):
    lefts, hidden, grad = refs[:4], refs[4:8], refs[8]
    left_ref, local_ref, gram_ref = refs[9:]
    total = jnp.zeros((TOKENS + RANK, RANK), F32)
    for r in range(4):
        for p in range(4):
            here = pl.ds(pl.multiple_of(table[4 * r + p] * BLOCK, 128), BLOCK)
            block = lefts[r][p]
            total += dot(jnp.concatenate([h[:, here] for h in hidden] + [block], axis=0), block, 1, 1)
            left_ref[:, here] = block
    gram_ref[...] = total[TOKENS:]
    local_ref[...] = sum(dot(t, grad[...], 0, 0) for t in reversed(thirds(total[:TOKENS])))


def eliminate(both, first, last):
    row_of = lax.broadcasted_iota(jnp.int32, (RANK, 1), 0)
    for k in range(first, last):
        pivot = both[k : k + 1, k : k + 1]
        factor = jnp.where(row_of > k, both[:, k : k + 1] / pivot, 0.0)
        scale = jnp.where(row_of == k, lax.rsqrt(pivot), 1.0)
        both = both * scale - factor * both[k : k + 1, :]
    return both


def upper_kernel(gram, out_ref):
    eye = lax.broadcasted_iota(jnp.int32, (RANK, RANK), 0) == lax.broadcasted_iota(jnp.int32, (RANK, RANK), 1)
    out_ref[...] = eliminate(jnp.concatenate([gram[...], eye.astype(F32)], axis=1), 0, RANK // 2)


def lower_kernel(both, out_ref):
    out_ref[...] = eliminate(both[...], RANK // 2, RANK)[:, RANK:]


def error_kernel(inverse, s0, s1, s2, s3, grad, left, h0, h1, h2, h3, right_ref, out_ref, weights):
    @pl.when(pl.program_id(0) == 0)
    def _():
        summed = (s0[...] + s1[...]) + (s2[...] + s3[...])
        inv = inverse[...]
        right = lax.dot_general(
            inv, summed, (((1,), (0,)), ((), ())), precision=HIGH, preferred_element_type=F32
        ) * (1.0 / 16)
        right_ref[...] = right
        m = -lax.dot_general(inv, right, (((0,), (0,)), ((), ())), precision=HIGH, preferred_element_type=F32)
        high = m.astype(BF)
        weights[:TOKENS, :] = grad[...]
        weights[TOKENS : TOKENS + RANK, :] = high
        weights[TOKENS + RANK :, :] = (m - high.astype(F32)).astype(BF)

    block = left[...]
    rows = jnp.concatenate([h0[...], h1[...], h2[...], h3[...], block, block], axis=0)
    out_ref[...] = dot(rows, weights[...], 0, 0).astype(BF)


def error_of(inverse, sums, grad, left, hidden):
    def whole(a):
        return pl.BlockSpec(a.shape, lambda i: (0, 0))

    def some(a):
        return pl.BlockSpec((a.shape[0], STEP), lambda i: (0, i))

    return pl.pallas_call(
        error_kernel,
        out_shape=(jax.ShapeDtypeStruct((RANK, COLS), F32), jax.ShapeDtypeStruct((F, COLS), BF)),
        grid=(F // STEP,),
        in_specs=[whole(inverse)] + [whole(s) for s in sums] + [whole(grad), some(left)] + [some(h) for h in hidden],
        out_specs=(
            pl.BlockSpec((RANK, COLS), lambda i: (0, 0)),
            pl.BlockSpec((STEP, COLS), lambda i: (i, 0)),
        ),
        scratch_shapes=[pltpu.VMEM((TOKENS + 2 * RANK, COLS), BF)],
        compiler_params=LIMIT,
        cost_estimate=pl.CostEstimate(
            flops=2 * (TOKENS + 2 * RANK) * F * COLS,
            bytes_accessed=2 * (TOKENS + RANK + COLS) * F,
            transcendentals=0,
        ),
        name="error_new",
    )(inverse, *sums, grad, left, *hidden)


def input_kernel(group, shard, t0, t1, t2, t3, near, far, out_ref):
    total = jnp.zeros((TOKENS, PART), F32)
    for d in range(16):
        rows = jnp.concatenate([t[:, shard[d]].reshape(64, COLS) for t in (t0, t1, t2, t3)], axis=0)
        total += dot(rows, near[d] if d < 8 else far[d - 8], 1, 1)
    total = total.astype(BF).reshape(16, 16, PART)
    for i in range(16):
        out_ref[group[i]] = total[i]


def input_of(group, shard, tokens, near, far):
    return pl.pallas_call(
        input_kernel,
        out_shape=jax.ShapeDtypeStruct((16, 16, BLOCK), BF),
        grid=(BLOCK // PART,),
        in_specs=[SMEM, SMEM]
        + [pl.BlockSpec(t.shape, lambda i: (0, 0, 0, 0)) for t in tokens]
        + [pl.BlockSpec((8, PART, COLS), lambda i: (0, i, 0))] * 2,
        out_specs=pl.BlockSpec((16, 16, PART), lambda i: (0, 0, i)),
        compiler_params=pltpu.CompilerParams(vmem_limit_bytes=56 * 2**20),
        cost_estimate=pl.CostEstimate(
            flops=2 * TOKENS * 16 * COLS * BLOCK, bytes_accessed=10 * 2**20, transcendentals=0
        ),
        name="input_grad",
    )(group, shard, *tokens, near, far)


def on_device(hidden_rows, out_grad, down_weight, query_init):
    zl, x, y, zh, c = (lax.axis_index(a) for a in AXES)
    four = jnp.arange(4)
    ahead = (y + four) % 4
    grad = out_grad[0]
    mine = hidden_rows[0]

    with jax.named_scope("prepare"):
        order = jnp.concatenate([ahead * 4 + h * 2 + k for k in (c, 1 - c) for h in (zh, 1 - zh)]).astype(jnp.int32)
        grad_rows, a = call(
            prepare_kernel,
            [((TOKENS, COLS), BF), ((2 * RANK, TOKENS), BF)],
            [order],
            [grad.reshape(16, 16, COLS), query_init],
            2 * 3 * RANK * TOKENS * COLS,
            "prepare",
        )

    with jax.named_scope("hidden_gather"):
        other = lax.ppermute(mine, "zh", SWAP)
        near = jnp.concatenate([mine] + ring3(mine, "y"), axis=0)
    with jax.named_scope("grad_gather"):
        tokens = lax.all_to_all(grad.reshape(16, 16, COLS), ("y", "zh", "c"), 0, 0)
    near, other, tokens, a = lax.optimization_barrier((near, other, tokens, a))
    with jax.named_scope("weight_gather"):
        weight = lax.all_gather(down_weight, ("y", "c"))
        far_weight = lax.ppermute(after(down_weight, near), "zh", SWAP)
    with jax.named_scope("hidden_gather"):
        far = jnp.concatenate([other] + ring3(other, "y"), axis=0)
        cross = lax.ppermute(near, "c", SWAP)
        far, far_weight, cross = lax.optimization_barrier((far, far_weight, cross))
        hidden = [near, far, cross, lax.ppermute(far, "c", SWAP)]
    with jax.named_scope("weight_gather"):
        far_weight = lax.all_gather(far_weight, ("y", "c"))

    table = (((x + four) % 4)[:, None] * 4 + (zl ^ four)[None, :]).reshape(16).astype(jnp.int32)
    with jax.named_scope("left_reduce"):
        parts = call(
            left_kernel,
            [((4, RANK, BLOCK), BF)] * 4,
            [table],
            [a, *hidden],
            2 * 2 * RANK * TOKENS * F,
            "left",
        )
        parts = [parts[0]] + [lax.ppermute(parts[r], "x", shift(r)) for r in (1, 2, 3)]
        tokens = jnp.stack([tokens] + flip3(after(tokens, parts[0])))
        parts, tokens = lax.optimization_barrier((parts, tokens))
        block, *sends = call(
            sum_kernel,
            [((RANK, BLOCK), F32)] + [((RANK, BLOCK), BF)] * 3,
            [],
            parts,
            16 * RANK * BLOCK,
            "sum",
        )
        ready = after(tokens, sends[0])
        token1, token3 = (lax.ppermute(ready, "x", shift(-s)) for s in (1, 3))
        for s in (1, 2, 3):
            block = block + lax.ppermute(sends[s - 1], "zl", flip(s)).astype(F32)
        block, token1, token3 = lax.optimization_barrier(((block * (1.0 / 16)).astype(BF), token1, token3))
    with jax.named_scope("left_gather"):
        token2 = lax.ppermute(after(tokens, block), "x", shift(-2))
        column = jnp.stack([block] + flip3(block))
        column, token2 = lax.optimization_barrier((column, token2))
        lefts = [column] + ring3(column, "x")

    with jax.named_scope("input_grad"):
        group = ((zl ^ four)[None, :] * 4 + ((x + four) % 4)[:, None]).reshape(16).astype(jnp.int32)
        both = jnp.arange(8)
        shard = [(both // 2) * 4 + h * 2 + both % 2 for h in (zh, 1 - zh)]
        shard = jnp.concatenate(shard).astype(jnp.int32)
        partial = input_of(group, shard, [after(tokens, column), token1, token2, token3], weight, far_weight)
        lefts, _ = lax.optimization_barrier((lefts, partial))

    with jax.named_scope("stats"):
        left, local, gram = call(
            stats_kernel,
            [((RANK, F), BF), ((RANK, COLS), F32), ((RANK, RANK), F32)],
            [table],
            [*lefts, *hidden, grad_rows],
            2 * RANK * (TOKENS + RANK) * F,
            "stats",
        )
    with jax.named_scope("right"):
        half = call(upper_kernel, [((RANK, 2 * RANK), F32)], [], [gram], 64 * 64 * 128, "inverse_upper")[0]
        for v in ring3(local, "x"):
            local = local + v
        local, half = lax.optimization_barrier((local, half))
        sums = [local] + flip3(local)
        inverse = call(lower_kernel, [((RANK, RANK), F32)], [], [half], 64 * 64 * 128, "inverse_lower")[0]
    with jax.named_scope("error_new"):
        right, error_new = error_of(inverse, sums, grad_rows, left, hidden)

    with jax.named_scope("input_grad"):
        summed = lax.all_to_all(partial, ("zl", "x"), 0, 0)
        input_grad = call(lay_kernel, [((16, F), BF)], [], [summed], 16 * F, "lay")[0][None]
    return input_grad, right, error_new[None]


def solution(mesh):
    fine = Mesh(mesh.devices.reshape(SIZES), AXES)
    dp, tensor = ("zl", "x"), ("y", "zh", "c")
    return jax.shard_map(
        on_device,
        mesh=fine,
        in_specs=(P(dp, tensor, None), P(dp, None, tensor), P(dp, tensor), P(None, tensor)),
        out_specs=(P(dp, tensor, None), P(None, tensor), P(dp, None, tensor)),
        check_vma=False,
    )
```

```python
import functools

import jax
import jax.numpy as jnp
from jax import lax
from jax.experimental import pallas as pl
from jax.experimental.pallas import tpu as pltpu
from jax.sharding import Mesh
from jax.sharding import PartitionSpec as P

AXES = ("zl", "x", "y", "zh", "c")
SIZES = (4, 4, 4, 2, 2)
F = 14336
BLOCK = 896
RANK = 64
TOKENS = 256
COLS = 256
STEP = 3584
PART = 128
BF = jnp.bfloat16
F32 = jnp.float32
HIGH = lax.Precision.HIGHEST
SWAP = ((0, 1), (1, 0))
VMEM = pl.BlockSpec(memory_space=pltpu.VMEM)
SMEM = pl.BlockSpec(memory_space=pltpu.SMEM)
LIMIT = pltpu.CompilerParams(vmem_limit_bytes=24 * 2**20)


def shift(s):
    return tuple((i, (i + s) % 4) for i in range(4))


def flip(s):
    return tuple((i, i ^ s) for i in range(4))


def ring3(value, axis):
    return [lax.ppermute(value, axis, shift(-s)) for s in (1, 2, 3)]


def flip3(value):
    return [lax.ppermute(value, "zl", flip(s)) for s in (1, 2, 3)]


def after(value, *others):
    return lax.optimization_barrier((value, *others))[0]


def dot(a, b, ca, cb):
    return lax.dot_general(a, b, (((ca,), (cb,)), ((), ())), preferred_element_type=F32)


def thirds(value):
    parts = []
    for _ in range(3):
        parts.append(value.astype(BF))
        value = value - parts[-1].astype(F32)
    return parts


def call(kernel, shapes, tables, arrays, flops, name):
    nbytes = sum(a.size * a.dtype.itemsize for a in arrays)
    return pl.pallas_call(
        kernel,
        out_shape=[jax.ShapeDtypeStruct(s, d) for s, d in shapes],
        in_specs=[SMEM] * len(tables) + [VMEM] * len(arrays),
        out_specs=[VMEM] * len(shapes),
        compiler_params=LIMIT,
        cost_estimate=pl.CostEstimate(flops=flops, bytes_accessed=nbytes, transcendentals=0),
        name=name,
    )(*tables, *arrays)


def prepare_kernel(order, grad, query, rows_ref, a_ref):
    for i in range(16):
        rows_ref[16 * i : 16 * i + 16, :] = grad[order[i]]
    rows = rows_ref[...]
    a = sum(dot(q, rows, 1, 1) for q in reversed(thirds(query[...])))
    high = a.astype(BF)
    a_ref[:RANK, :] = high
    a_ref[RANK:, :] = (a - high.astype(F32)).astype(BF)


def lay_kernel(blocks, out_ref):
    for j in range(16):
        out_ref[:, BLOCK * j : BLOCK * (j + 1)] = blocks[j]


def left_kernel(table, a_ref, *refs):
    hidden, outs = refs[:4], refs[4:]
    a = a_ref[...]
    for r in range(4):
        for p in range(4):
            here = pl.ds(pl.multiple_of(table[4 * r + p] * BLOCK, 128), BLOCK)
            both = dot(a, jnp.concatenate([h[:, here] for h in hidden], axis=0), 1, 0)
            outs[r][p] = (both[:RANK] + both[RANK:]).astype(BF)


def sum_kernel(a, b, c, d, own, *outs):
    for p in range(4):
        total = (a[p].astype(F32) + b[p].astype(F32)) + (c[p].astype(F32) + d[p].astype(F32))
        if p == 0:
            own[...] = total
        else:
            outs[p - 1][...] = total.astype(BF)


def stats_kernel(table, *refs):
    lefts, hidden, grad = refs[:4], refs[4:8], refs[8]
    left_ref, local_ref, gram_ref = refs[9:]
    total = jnp.zeros((TOKENS + RANK, RANK), F32)
    for r in range(4):
        for p in range(4):
            here = pl.ds(pl.multiple_of(table[4 * r + p] * BLOCK, 128), BLOCK)
            block = lefts[r][p]
            total += dot(jnp.concatenate([h[:, here] for h in hidden] + [block], axis=0), block, 1, 1)
            left_ref[:, here] = block
    gram_ref[...] = total[TOKENS:]
    local_ref[...] = sum(dot(t, grad[...], 0, 0) for t in reversed(thirds(total[:TOKENS])))


def eliminate(both, first, last):
    row_of = lax.broadcasted_iota(jnp.int32, (RANK, 1), 0)
    for k in range(first, last):
        pivot = both[k : k + 1, k : k + 1]
        factor = jnp.where(row_of > k, both[:, k : k + 1] / pivot, 0.0)
        scale = jnp.where(row_of == k, lax.rsqrt(pivot), 1.0)
        both = both * scale - factor * both[k : k + 1, :]
    return both


def upper_kernel(gram, out_ref):
    eye = lax.broadcasted_iota(jnp.int32, (RANK, RANK), 0) == lax.broadcasted_iota(jnp.int32, (RANK, RANK), 1)
    out_ref[...] = eliminate(jnp.concatenate([gram[...], eye.astype(F32)], axis=1), 0, RANK // 2)


def lower_kernel(both, out_ref):
    out_ref[...] = eliminate(both[...], RANK // 2, RANK)[:, RANK:]


def error_kernel(inverse, s0, s1, s2, s3, grad, left, h0, h1, h2, h3, right_ref, out_ref, weights):
    @pl.when(pl.program_id(0) == 0)
    def _():
        summed = (s0[...] + s1[...]) + (s2[...] + s3[...])
        inv = inverse[...]
        right = lax.dot_general(
            inv, summed, (((1,), (0,)), ((), ())), precision=HIGH, preferred_element_type=F32
        ) * (1.0 / 16)
        right_ref[...] = right
        m = -lax.dot_general(inv, right, (((0,), (0,)), ((), ())), precision=HIGH, preferred_element_type=F32)
        high = m.astype(BF)
        weights[:TOKENS, :] = grad[...]
        weights[TOKENS : TOKENS + RANK, :] = high
        weights[TOKENS + RANK :, :] = (m - high.astype(F32)).astype(BF)

    block = left[...]
    rows = jnp.concatenate([h0[...], h1[...], h2[...], h3[...], block, block], axis=0)
    out_ref[...] = dot(rows, weights[...], 0, 0).astype(BF)


def error_of(inverse, sums, grad, left, hidden):
    def whole(a):
        return pl.BlockSpec(a.shape, lambda i: (0, 0))

    def some(a):
        return pl.BlockSpec((a.shape[0], STEP), lambda i: (0, i))

    return pl.pallas_call(
        error_kernel,
        out_shape=(jax.ShapeDtypeStruct((RANK, COLS), F32), jax.ShapeDtypeStruct((F, COLS), BF)),
        grid=(F // STEP,),
        in_specs=[whole(inverse)] + [whole(s) for s in sums] + [whole(grad), some(left)] + [some(h) for h in hidden],
        out_specs=(
            pl.BlockSpec((RANK, COLS), lambda i: (0, 0)),
            pl.BlockSpec((STEP, COLS), lambda i: (i, 0)),
        ),
        scratch_shapes=[pltpu.VMEM((TOKENS + 2 * RANK, COLS), BF)],
        compiler_params=LIMIT,
        cost_estimate=pl.CostEstimate(
            flops=2 * (TOKENS + 2 * RANK) * F * COLS,
            bytes_accessed=2 * (TOKENS + RANK + COLS) * F,
            transcendentals=0,
        ),
        name="error_new",
    )(inverse, *sums, grad, left, *hidden)


def input_kernel(group, shard, t0, t1, t2, t3, near, far, out_ref):
    total = jnp.zeros((TOKENS, PART), F32)
    for d in range(16):
        rows = jnp.concatenate([t[:, shard[d]].reshape(64, COLS) for t in (t0, t1, t2, t3)], axis=0)
        total += dot(rows, near[d] if d < 8 else far[d - 8], 1, 1)
    total = total.astype(BF).reshape(16, 16, PART)
    for i in range(16):
        out_ref[group[i]] = total[i]


def input_of(group, shard, tokens, near, far):
    return pl.pallas_call(
        input_kernel,
        out_shape=jax.ShapeDtypeStruct((16, 16, BLOCK), BF),
        grid=(BLOCK // PART,),
        in_specs=[SMEM, SMEM]
        + [pl.BlockSpec(t.shape, lambda i: (0, 0, 0, 0)) for t in tokens]
        + [pl.BlockSpec((8, PART, COLS), lambda i: (0, i, 0))] * 2,
        out_specs=pl.BlockSpec((16, 16, PART), lambda i: (0, 0, i)),
        compiler_params=pltpu.CompilerParams(vmem_limit_bytes=56 * 2**20),
        cost_estimate=pl.CostEstimate(
            flops=2 * TOKENS * 16 * COLS * BLOCK, bytes_accessed=10 * 2**20, transcendentals=0
        ),
        name="input_grad",
    )(group, shard, *tokens, near, far)


def on_device(hidden_rows, out_grad, down_weight, query_init):
    zl, x, y, zh, c = (lax.axis_index(a) for a in AXES)
    four = jnp.arange(4)
    ahead = (y + four) % 4
    grad = out_grad[0]
    mine = hidden_rows[0]

    with jax.named_scope("prepare"):
        order = jnp.concatenate([ahead * 4 + h * 2 + k for k in (c, 1 - c) for h in (zh, 1 - zh)]).astype(jnp.int32)
        grad_rows, a = call(
            prepare_kernel,
            [((TOKENS, COLS), BF), ((2 * RANK, TOKENS), BF)],
            [order],
            [grad.reshape(16, 16, COLS), query_init],
            2 * 3 * RANK * TOKENS * COLS,
            "prepare",
        )

    with jax.named_scope("hidden_gather"):
        other = lax.ppermute(mine, "zh", SWAP)
        near = jnp.concatenate([mine] + ring3(mine, "y"), axis=0)
    with jax.named_scope("grad_gather"):
        tokens = lax.all_to_all(grad.reshape(16, 16, COLS), ("y", "zh", "c"), 0, 0)
    near, other, a = lax.optimization_barrier((near, other, a))
    with jax.named_scope("weight_gather"):
        far_weight = lax.ppermute(after(down_weight, near), "zh", SWAP)
    with jax.named_scope("hidden_gather"):
        far = jnp.concatenate([other] + ring3(other, "y"), axis=0)
        shared, tokens = lax.optimization_barrier((near, tokens))
        cross = lax.ppermute(shared, "c", SWAP)
        far, far_weight, cross = lax.optimization_barrier((far, far_weight, cross))
        hidden = [near, far, cross, lax.ppermute(far, "c", SWAP)]
    with jax.named_scope("weight_gather"):
        weight = lax.all_gather(after(down_weight, far), ("y", "c"))
        far_weight = lax.all_gather(far_weight, ("y", "c"))

    table = (((x + four) % 4)[:, None] * 4 + (zl ^ four)[None, :]).reshape(16).astype(jnp.int32)
    with jax.named_scope("left_reduce"):
        parts = call(
            left_kernel,
            [((4, RANK, BLOCK), BF)] * 4,
            [table],
            [a, *hidden],
            2 * 2 * RANK * TOKENS * F,
            "left",
        )
        parts = [parts[0]] + [lax.ppermute(parts[r], "x", shift(r)) for r in (1, 2, 3)]
        tokens = jnp.stack([tokens] + flip3(after(tokens, parts[0])))
        parts, tokens = lax.optimization_barrier((parts, tokens))
        block, *sends = call(
            sum_kernel,
            [((RANK, BLOCK), F32)] + [((RANK, BLOCK), BF)] * 3,
            [],
            parts,
            16 * RANK * BLOCK,
            "sum",
        )
        ready = after(tokens, sends[0])
        token1, token3 = (lax.ppermute(ready, "x", shift(-s)) for s in (1, 3))
        for s in (1, 2, 3):
            block = block + lax.ppermute(sends[s - 1], "zl", flip(s)).astype(F32)
        block, token1, token3 = lax.optimization_barrier(((block * (1.0 / 16)).astype(BF), token1, token3))
    with jax.named_scope("left_gather"):
        token2 = lax.ppermute(after(tokens, block), "x", shift(-2))
        column = jnp.stack([block] + flip3(block))
        column, token2 = lax.optimization_barrier((column, token2))
        lefts = [column] + ring3(column, "x")

    with jax.named_scope("input_grad"):
        group = ((zl ^ four)[None, :] * 4 + ((x + four) % 4)[:, None]).reshape(16).astype(jnp.int32)
        both = jnp.arange(8)
        shard = [(both // 2) * 4 + h * 2 + both % 2 for h in (zh, 1 - zh)]
        shard = jnp.concatenate(shard).astype(jnp.int32)
        partial = input_of(group, shard, [after(tokens, column), token1, token2, token3], weight, far_weight)
        lefts, _ = lax.optimization_barrier((lefts, partial))

    with jax.named_scope("stats"):
        left, local, gram = call(
            stats_kernel,
            [((RANK, F), BF), ((RANK, COLS), F32), ((RANK, RANK), F32)],
            [table],
            [*lefts, *hidden, grad_rows],
            2 * RANK * (TOKENS + RANK) * F,
            "stats",
        )
    with jax.named_scope("right"):
        half = call(upper_kernel, [((RANK, 2 * RANK), F32)], [], [gram], 64 * 64 * 128, "inverse_upper")[0]
        for v in ring3(local, "x"):
            local = local + v
        local, half = lax.optimization_barrier((local, half))
        sums = [local] + flip3(local)
        inverse = call(lower_kernel, [((RANK, RANK), F32)], [], [half], 64 * 64 * 128, "inverse_lower")[0]
    with jax.named_scope("error_new"):
        right, error_new = error_of(inverse, sums, grad_rows, left, hidden)

    with jax.named_scope("input_grad"):
        summed = lax.all_to_all(partial, ("zl", "x"), 0, 0)
        input_grad = call(lay_kernel, [((16, F), BF)], [], [summed], 16 * F, "lay")[0][None]
    return input_grad, right, error_new[None]


def solution(mesh):
    fine = Mesh(mesh.devices.reshape(SIZES), AXES)
    dp, tensor = ("zl", "x"), ("y", "zh", "c")
    return jax.shard_map(
        on_device,
        mesh=fine,
        in_specs=(P(dp, tensor, None), P(dp, None, tensor), P(dp, tensor), P(None, tensor)),
        out_specs=(P(dp, tensor, None), P(None, tensor), P(dp, None, tensor)),
        check_vma=False,
    )
```

```python
import functools

import jax
import jax.numpy as jnp
from jax import lax
from jax.experimental import pallas as pl
from jax.experimental.pallas import tpu as pltpu
from jax.sharding import Mesh
from jax.sharding import PartitionSpec as P

AXES = ("zl", "x", "y", "zh", "c")
SIZES = (4, 4, 4, 2, 2)
F = 14336
BLOCK = 896
RANK = 64
TOKENS = 256
COLS = 256
STEP = 3584
PART = 128
BF = jnp.bfloat16
F32 = jnp.float32
HIGH = lax.Precision.HIGHEST
SWAP = ((0, 1), (1, 0))
VMEM = pl.BlockSpec(memory_space=pltpu.VMEM)
SMEM = pl.BlockSpec(memory_space=pltpu.SMEM)
LIMIT = pltpu.CompilerParams(vmem_limit_bytes=24 * 2**20)


def shift(s):
    return tuple((i, (i + s) % 4) for i in range(4))


def flip(s):
    return tuple((i, i ^ s) for i in range(4))


def ring3(value, axis):
    return [lax.ppermute(value, axis, shift(-s)) for s in (1, 2, 3)]


def flip3(value):
    return [lax.ppermute(value, "zl", flip(s)) for s in (1, 2, 3)]


def after(value, *others):
    return lax.optimization_barrier((value, *others))[0]


def dot(a, b, ca, cb):
    return lax.dot_general(a, b, (((ca,), (cb,)), ((), ())), preferred_element_type=F32)


def thirds(value):
    parts = []
    for _ in range(3):
        parts.append(value.astype(BF))
        value = value - parts[-1].astype(F32)
    return parts


def call(kernel, shapes, tables, arrays, flops, name):
    nbytes = sum(a.size * a.dtype.itemsize for a in arrays)
    return pl.pallas_call(
        kernel,
        out_shape=[jax.ShapeDtypeStruct(s, d) for s, d in shapes],
        in_specs=[SMEM] * len(tables) + [VMEM] * len(arrays),
        out_specs=[VMEM] * len(shapes),
        compiler_params=LIMIT,
        cost_estimate=pl.CostEstimate(flops=flops, bytes_accessed=nbytes, transcendentals=0),
        name=name,
    )(*tables, *arrays)


def prepare_kernel(order, grad, query, rows_ref, a_ref):
    for i in range(16):
        rows_ref[16 * i : 16 * i + 16, :] = grad[order[i]]
    rows = rows_ref[...]
    a = sum(dot(q, rows, 1, 1) for q in reversed(thirds(query[...])))
    high = a.astype(BF)
    a_ref[:RANK, :] = high
    a_ref[RANK:, :] = (a - high.astype(F32)).astype(BF)


def left_kernel(table, a_ref, *refs):
    hidden, outs = refs[:4], refs[4:]
    a = a_ref[...]
    for r in range(4):
        for p in range(4):
            here = pl.ds(pl.multiple_of(table[4 * r + p] * BLOCK, 128), BLOCK)
            both = dot(a, jnp.concatenate([h[:, here] for h in hidden], axis=0), 1, 0)
            outs[r][p] = (both[:RANK] + both[RANK:]).astype(BF)


def sum_kernel(a, b, c, d, own, *outs):
    for p in range(4):
        total = (a[p].astype(F32) + b[p].astype(F32)) + (c[p].astype(F32) + d[p].astype(F32))
        if p == 0:
            own[...] = total
        else:
            outs[p - 1][...] = total.astype(BF)


def stats_kernel(table, *refs):
    lefts, hidden, grad = refs[:4], refs[4:8], refs[8]
    left_ref, local_ref, gram_ref = refs[9:]
    total = jnp.zeros((TOKENS + RANK, RANK), F32)
    for r in range(4):
        for p in range(4):
            here = pl.ds(pl.multiple_of(table[4 * r + p] * BLOCK, 128), BLOCK)
            block = lefts[r][p]
            total += dot(jnp.concatenate([h[:, here] for h in hidden] + [block], axis=0), block, 1, 1)
            left_ref[:, here] = block
    gram_ref[...] = total[TOKENS:]
    local_ref[...] = sum(dot(t, grad[...], 0, 0) for t in reversed(thirds(total[:TOKENS])))


def eliminate(both, first, last):
    row_of = lax.broadcasted_iota(jnp.int32, (RANK, 1), 0)
    for k in range(first, last):
        pivot = both[k : k + 1, k : k + 1]
        factor = jnp.where(row_of > k, both[:, k : k + 1] / pivot, 0.0)
        scale = jnp.where(row_of == k, lax.rsqrt(pivot), 1.0)
        both = both * scale - factor * both[k : k + 1, :]
    return both


def upper_kernel(gram, out_ref):
    eye = lax.broadcasted_iota(jnp.int32, (RANK, RANK), 0) == lax.broadcasted_iota(jnp.int32, (RANK, RANK), 1)
    out_ref[...] = eliminate(jnp.concatenate([gram[...], eye.astype(F32)], axis=1), 0, RANK // 2)


def lower_kernel(both, out_ref, square_ref):
    inverse = eliminate(both[...], RANK // 2, RANK)[:, RANK:]
    out_ref[...] = inverse
    square_ref[...] = lax.dot_general(
        inverse, inverse, (((0,), (0,)), ((), ())), precision=HIGH, preferred_element_type=F32
    )


def error_kernel(
    inverse, square, s0, s1, s2, s3, grad, blocks, left, h0, h1, h2, h3, right_ref, out_ref, laid_ref, weights
):
    @pl.when(pl.program_id(0) == 0)
    def _():
        summed = ((s0[...] + s1[...]) + (s2[...] + s3[...])) * (1.0 / 16)
        right_ref[...] = lax.dot_general(
            inverse[...], summed, (((1,), (0,)), ((), ())), precision=HIGH, preferred_element_type=F32
        )
        m = -lax.dot_general(
            square[...], summed, (((1,), (0,)), ((), ())), precision=HIGH, preferred_element_type=F32
        )
        high = m.astype(BF)
        weights[:TOKENS, :] = grad[...]
        weights[TOKENS : TOKENS + RANK, :] = high
        weights[TOKENS + RANK :, :] = (m - high.astype(F32)).astype(BF)

    for j in range(STEP // BLOCK):
        laid_ref[:, BLOCK * j : BLOCK * (j + 1)] = blocks[j]
    block = left[...]
    rows = jnp.concatenate([h0[...], h1[...], h2[...], h3[...], block, block], axis=0)
    out_ref[...] = dot(rows, weights[...], 0, 0).astype(BF)


def error_of(inverse, square, sums, grad, blocks, left, hidden):
    def whole(a):
        return pl.BlockSpec(a.shape, lambda i: (0, 0))

    def some(a):
        return pl.BlockSpec((a.shape[0], STEP), lambda i: (0, i))

    return pl.pallas_call(
        error_kernel,
        out_shape=(
            jax.ShapeDtypeStruct((RANK, COLS), F32),
            jax.ShapeDtypeStruct((F, COLS), BF),
            jax.ShapeDtypeStruct((16, F), BF),
        ),
        grid=(F // STEP,),
        in_specs=[whole(inverse), whole(square)]
        + [whole(s) for s in sums]
        + [whole(grad), pl.BlockSpec((STEP // BLOCK, 16, BLOCK), lambda i: (i, 0, 0)), some(left)]
        + [some(h) for h in hidden],
        out_specs=(
            pl.BlockSpec((RANK, COLS), lambda i: (0, 0)),
            pl.BlockSpec((STEP, COLS), lambda i: (i, 0)),
            pl.BlockSpec((16, STEP), lambda i: (0, i)),
        ),
        scratch_shapes=[pltpu.VMEM((TOKENS + 2 * RANK, COLS), BF)],
        compiler_params=LIMIT,
        cost_estimate=pl.CostEstimate(
            flops=2 * (TOKENS + 2 * RANK) * F * COLS,
            bytes_accessed=2 * (TOKENS + RANK + COLS) * F,
            transcendentals=0,
        ),
        name="error_new",
    )(inverse, square, *sums, grad, blocks, left, *hidden)


def input_kernel(group, shard, t0, t1, t2, t3, near, far, out_ref):
    total = jnp.zeros((TOKENS, PART), F32)
    for d in range(16):
        rows = jnp.concatenate([t[:, shard[d]].reshape(64, COLS) for t in (t0, t1, t2, t3)], axis=0)
        total += dot(rows, near[d] if d < 8 else far[d - 8], 1, 1)
    total = total.astype(BF).reshape(16, 16, PART)
    for i in range(16):
        out_ref[group[i]] = total[i]


def input_of(group, shard, tokens, near, far):
    return pl.pallas_call(
        input_kernel,
        out_shape=jax.ShapeDtypeStruct((16, 16, BLOCK), BF),
        grid=(BLOCK // PART,),
        in_specs=[SMEM, SMEM]
        + [pl.BlockSpec(t.shape, lambda i: (0, 0, 0, 0)) for t in tokens]
        + [pl.BlockSpec((8, PART, COLS), lambda i: (0, i, 0))] * 2,
        out_specs=pl.BlockSpec((16, 16, PART), lambda i: (0, 0, i)),
        compiler_params=pltpu.CompilerParams(vmem_limit_bytes=56 * 2**20),
        cost_estimate=pl.CostEstimate(
            flops=2 * TOKENS * 16 * COLS * BLOCK, bytes_accessed=10 * 2**20, transcendentals=0
        ),
        name="input_grad",
    )(group, shard, *tokens, near, far)


def on_device(hidden_rows, out_grad, down_weight, query_init):
    zl, x, y, zh, c = (lax.axis_index(a) for a in AXES)
    four = jnp.arange(4)
    ahead = (y + four) % 4
    grad = out_grad[0]
    mine = hidden_rows[0]

    with jax.named_scope("prepare"):
        order = jnp.concatenate([ahead * 4 + h * 2 + k for k in (c, 1 - c) for h in (zh, 1 - zh)]).astype(jnp.int32)
        grad_rows, a = call(
            prepare_kernel,
            [((TOKENS, COLS), BF), ((2 * RANK, TOKENS), BF)],
            [order],
            [grad.reshape(16, 16, COLS), query_init],
            2 * 3 * RANK * TOKENS * COLS,
            "prepare",
        )

    with jax.named_scope("hidden_gather"):
        other = lax.ppermute(mine, "zh", SWAP)
        near = jnp.concatenate([mine] + ring3(mine, "y"), axis=0)
    with jax.named_scope("grad_gather"):
        tokens = lax.all_to_all(grad.reshape(16, 16, COLS), ("y", "zh", "c"), 0, 0)
    near, other, a = lax.optimization_barrier((near, other, a))
    with jax.named_scope("weight_gather"):
        far_weight = lax.ppermute(after(down_weight, near), "zh", SWAP)
    with jax.named_scope("hidden_gather"):
        far = jnp.concatenate([other] + ring3(other, "y"), axis=0)
        shared, tokens = lax.optimization_barrier((near, tokens))
        cross = lax.ppermute(shared, "c", SWAP)
        far, far_weight, cross = lax.optimization_barrier((far, far_weight, cross))
        hidden = [near, far, cross, lax.ppermute(far, "c", SWAP)]
    with jax.named_scope("weight_gather"):
        weight = lax.all_gather(after(down_weight, far), ("y", "c"))
        far_weight = lax.all_gather(far_weight, ("y", "c"))

    table = (((x + four) % 4)[:, None] * 4 + (zl ^ four)[None, :]).reshape(16).astype(jnp.int32)
    with jax.named_scope("left_reduce"):
        parts = call(
            left_kernel,
            [((4, RANK, BLOCK), BF)] * 4,
            [table],
            [a, *hidden],
            2 * 2 * RANK * TOKENS * F,
            "left",
        )
        parts = [parts[0]] + [lax.ppermute(parts[r], "x", shift(r)) for r in (1, 2, 3)]
        tokens = jnp.stack([tokens] + flip3(after(tokens, parts[0])))
        parts, tokens = lax.optimization_barrier((parts, tokens))
        block, *sends = call(
            sum_kernel,
            [((RANK, BLOCK), F32)] + [((RANK, BLOCK), BF)] * 3,
            [],
            parts,
            16 * RANK * BLOCK,
            "sum",
        )
        ready = after(tokens, sends[0])
        token1, token3 = (lax.ppermute(ready, "x", shift(-s)) for s in (1, 3))
        for s in (1, 2, 3):
            block = block + lax.ppermute(sends[s - 1], "zl", flip(s)).astype(F32)
        block, token1, token3 = lax.optimization_barrier(((block * (1.0 / 16)).astype(BF), token1, token3))
    with jax.named_scope("left_gather"):
        token2 = lax.ppermute(after(tokens, block), "x", shift(-2))
        column = jnp.stack([block] + flip3(block))
        column, token2 = lax.optimization_barrier((column, token2))
        lefts = [column] + ring3(column, "x")

    with jax.named_scope("input_grad"):
        group = ((zl ^ four)[None, :] * 4 + ((x + four) % 4)[:, None]).reshape(16).astype(jnp.int32)
        both = jnp.arange(8)
        shard = [(both // 2) * 4 + h * 2 + both % 2 for h in (zh, 1 - zh)]
        shard = jnp.concatenate(shard).astype(jnp.int32)
        partial = input_of(group, shard, [after(tokens, column), token1, token2, token3], weight, far_weight)
        lefts, _ = lax.optimization_barrier((lefts, partial))

    with jax.named_scope("stats"):
        left, local, gram = call(
            stats_kernel,
            [((RANK, F), BF), ((RANK, COLS), F32), ((RANK, RANK), F32)],
            [table],
            [*lefts, *hidden, grad_rows],
            2 * RANK * (TOKENS + RANK) * F,
            "stats",
        )
    with jax.named_scope("right"):
        half = call(upper_kernel, [((RANK, 2 * RANK), F32)], [], [gram], 64 * 64 * 128, "inverse_upper")[0]
        for v in ring3(local, "x"):
            local = local + v
        local, half = lax.optimization_barrier((local, half))
        sums = [local] + flip3(local)
        inverse, square = call(lower_kernel, [((RANK, RANK), F32)] * 2, [], [half], 64 * 64 * 128, "inverse_lower")
    with jax.named_scope("input_grad"):
        summed = lax.all_to_all(partial, ("zl", "x"), 0, 0)
    with jax.named_scope("error_new"):
        right, error_new, laid = error_of(inverse, square, sums, grad_rows, summed, left, hidden)
    return laid[None], right, error_new[None]


def solution(mesh):
    fine = Mesh(mesh.devices.reshape(SIZES), AXES)
    dp, tensor = ("zl", "x"), ("y", "zh", "c")
    return jax.shard_map(
        on_device,
        mesh=fine,
        in_specs=(P(dp, tensor, None), P(dp, None, tensor), P(dp, tensor), P(None, tensor)),
        out_specs=(P(dp, tensor, None), P(None, tensor), P(dp, None, tensor)),
        check_vma=False,
    )
```
